32 devices in a mesh: groups: 2 (over x), tensor: 16 (over z, y, core).
Axes of the slice: x: 2, y: 2, z: 4, core: 2. Of those that a mesh axis runs over, the one named last changes fastest.
Arguments:
- tokens: bfloat16 [256, 8192], P(('groups', 'tensor')), parts along dimension 0, may hold values from -6 to 6
- gate_matrix: bfloat16 [8192, 14336], P(None, 'tensor'), may hold values from -0.0625 to 0.0625
- up_matrix: bfloat16 [8192, 14336], P(None, 'tensor'), may hold values from -0.0625 to 0.0625
- adapter_input_maps: bfloat16 [16, 8192, 128], P('tensor'), may hold values from -0.0625 to 0.0625
- adapter_output_maps: bfloat16 [16, 2, 64, 14336], P(None, None, None, 'tensor'), may hold values from -0.75 to 0.75
- request_adapter: int32 [64, 1], P(('groups', 'tensor')), parts along dimension 0, may hold values from 0 to 15; in each aligned block of 32 rows (0 to 31, 32 to 63, ...) at most 8 rows name the same one
Outputs:
- hidden: bfloat16 [256, 14336], P('groups', 'tensor'), parts along dimension 0
The draws below stay inside these ranges and needn't reach their ends.
There are 2 independent parts, one for each index of `groups`. The reference program is written for one: setup_inputs(seed, part) draws one part's arguments, and reference() takes and returns one part's arrays. A program takes and returns all parts, laid end to end along the dimension named above; an argument that names none is the same for every part. Nothing has to cross between parts.
Inputs may be any that keep to these rules, and one draw needn't show every extreme that they name: `request_adapter`: no adapter is named by more than 8 requests, a bound that some block reaches; every adapter is named by some request.
All inputs are finite; a program needn't handle non-finite values.
Results may differ from the reference program's by a relative error of at most 0.0054.
Values may be sent and summed in bfloat16 or wider, within the bound.
A program may use at most 128 MiB of HBM per device.

```python
import math
import jax
import jax.numpy as jnp
import numpy as np
from jax import lax

MODEL_WIDTH = 8192
HIDDEN_UNITS = 14336
ADAPTER_RANK = 64
SEQ = 4
MOST = 8
TOKEN_TOTAL = 128
REQS = 32
ADAPTER_COUNT = 16


def steps_of(key, extent, pieces, smallest, high):
    def one(axis_at, shards_of):
        steps = jax.random.uniform(jax.random.fold_in(jax.random.fold_in(key, 6), axis_at), (shards_of,), jnp.float32, smallest / len(pieces), high / len(pieces))
        return jnp.repeat(jnp.exp(steps), extent[axis_at] // shards_of).reshape((-1,) + (1,) * (len(extent) - axis_at - 1))

    level = one(*pieces[0])
    for cut in pieces[1:]:
        level = level * one(*cut)
    return level


def routed_block(rng, own, number, rows, count, top, most, lean):
    order = jax.random.permutation(rng, count)
    heavy_load, ordinary = load_shares(count, rows * top, most, lean, True), load_shares(count, rows * top, most, lean, False)
    places = jnp.arange(count)

    def named(lengths, turn):
        used = int((lengths > 0).sum())
        fixed = max(1, used // 4)
        passed = fixed + (places - fixed + turn * (used - fixed)) % max(1, count - fixed)
        return jnp.zeros((count,), jnp.int32).at[order[jnp.where(places < fixed, places, passed)]].set(jnp.asarray(lengths, jnp.int32))

    lengths = jnp.where(number % 4 == 0, named(heavy_load, number // 4), named(ordinary, number - number // 4 - 1))
    mixed = jax.random.permutation(jax.random.fold_in(own, 3), count)
    donor, receiver = mixed[0:count // 2 * 2:2], mixed[1:count // 2 * 2:2]
    margin = jnp.minimum(lengths[donor] - 1, most - lengths[receiver]) // 2
    margin = jnp.where((donor == order[0]) | (receiver == order[0]) | (lengths[receiver] == 0), 0, jnp.maximum(margin, 0))
    passed = jax.random.randint(jax.random.fold_in(own, 4), (count // 2,), 0, 1 << 20) % (margin + 1)
    lengths = lengths.at[donor].add(-passed).at[receiver].add(passed)
    members = jnp.searchsorted(jnp.cumsum(lengths), jnp.arange(rows * top), side="right").astype(jnp.int32)
    grid = members.reshape(top, rows).T
    grid = grid[jax.random.permutation(jax.random.fold_in(own, 1), rows)]
    turn = jax.random.randint(jax.random.fold_in(own, 2), (rows, 1), 0, top)
    return jnp.take_along_axis(grid, (jnp.arange(top)[None, :] + turn) % top, axis=1)


def load_shares(number_of, total, most, lean, full):
    weights = [(1 << 20) // math.isqrt(standing ** lean) + 1 for standing in range(1, number_of + 1)]
    largest = most if full else min(most, max(-(-total // number_of), total * weights[0] // sum(weights)))
    least = 1 if total - largest >= number_of - 1 else 0
    holding, surplus = [largest] + [least] * (number_of - 1), total - largest - least * (number_of - 1)
    while surplus > 0:
        free = [i for i in range(1, number_of) if holding[i] < largest] or [i for i in range(1, number_of) if holding[i] < most]
        pool, budget = sum([weights[i] for i in free]), surplus
        for i in free:
            addition = min(most - holding[i], max(1, budget * weights[i] // pool), surplus)
            holding[i] = holding[i] + addition
            surplus = surplus - addition
    return np.array(holding)


def noise(rng, extent, spread, most, shards=(), dtype=jnp.bfloat16):
    level = steps_of(rng, extent, shards, -0.22, 0.18) if shards else 1.0
    result = jax.random.normal(rng, extent, jnp.float32) * spread * level
    return jnp.minimum(jnp.maximum(result, -most), most).astype(dtype)


def setup_inputs(seed: int = 0, part: int = 0) -> dict:
    key_list = jax.random.split(jax.random.key(seed), 7)
    own_keys = jax.random.split(jax.random.fold_in(key_list[6], part), 7)
    tokens = noise(own_keys[0], (TOKEN_TOTAL, MODEL_WIDTH), 1.0, 6.0, ((0, 16),))
    gate_matrix = noise(key_list[1], (MODEL_WIDTH, HIDDEN_UNITS), MODEL_WIDTH ** -0.5, 0.0625, ((1, 16),))
    up_matrix = noise(key_list[2], (MODEL_WIDTH, HIDDEN_UNITS), MODEL_WIDTH ** -0.5, 0.0625, ((1, 16),))
    adapter_input_maps = noise(key_list[3], (ADAPTER_COUNT, MODEL_WIDTH, 2 * ADAPTER_RANK), MODEL_WIDTH ** -0.5, 0.0625, ((0, 16),))
    adapter_output_maps = noise(key_list[4], (ADAPTER_COUNT, 2, ADAPTER_RANK, HIDDEN_UNITS), ADAPTER_RANK ** -0.5, 0.75, ((3, 16),))
    request_adapter_keys = jax.random.split(jax.random.fold_in(own_keys[5], 1), REQS // REQS)
    request_adapter_turns = jax.random.permutation(jax.random.fold_in(own_keys[5], 3), REQS // REQS)
    request_adapter = jax.vmap(lambda own, number: routed_block(jax.random.fold_in(own_keys[5], 2), own, number, REQS, ADAPTER_COUNT, 1, MOST, 2))(request_adapter_keys, request_adapter_turns).reshape((REQS, 1))
    return {"tokens": tokens, "gate_matrix": gate_matrix, "up_matrix": up_matrix, "adapter_input_maps": adapter_input_maps, "adapter_output_maps": adapter_output_maps, "request_adapter": request_adapter}


def reference(tokens, gate_matrix, up_matrix, adapter_input_maps, adapter_output_maps, request_adapter):
    gate_plain = jnp.dot(tokens, gate_matrix, preferred_element_type=jnp.float32)
    up_plain = jnp.dot(tokens, up_matrix, preferred_element_type=jnp.float32)
    adapter_table = request_adapter[:, 0].astype(jnp.int32)
    request_grouped = tokens.reshape(REQS, SEQ, MODEL_WIDTH)

    def request_split(item):
        token_rows, selected_adapter = item
        reduced_rank = jnp.dot(token_rows, adapter_input_maps[selected_adapter], preferred_element_type=jnp.float32).astype(jnp.bfloat16)
        gate_portion = jnp.dot(reduced_rank[:, :ADAPTER_RANK], adapter_output_maps[selected_adapter, 0], preferred_element_type=jnp.float32)
        up_portion = jnp.dot(reduced_rank[:, ADAPTER_RANK:], adapter_output_maps[selected_adapter, 1], preferred_element_type=jnp.float32)
        return gate_portion, up_portion

    gate_adapter_term, up_adapter_term = lax.map(request_split, (request_grouped, adapter_table))
    gate_output = gate_plain + gate_adapter_term.reshape(TOKEN_TOTAL, HIDDEN_UNITS)
    up_output = up_plain + up_adapter_term.reshape(TOKEN_TOTAL, HIDDEN_UNITS)
    return (jax.nn.silu(gate_output) * up_output).astype(jnp.bfloat16)
```

```python
import functools

import jax
import jax.numpy as jnp
from jax import lax
from jax.experimental import pallas as pl
from jax.experimental.pallas import tpu as pltpu
from jax.sharding import PartitionSpec as P

SEQ = 4
MOST = 8
LANES = 128
MESH = pl.DeviceIdType.MESH
F32 = jnp.float32
BF16 = jnp.bfloat16


def plan(chips, chunk):
    far, near = chips // 2, chips - 1 - chips // 2
    return (far, near) if chunk % 2 == 0 else (near, far)


def pieces_of(width):
    pieces = []
    full = width // 256 * 256 if width >= 256 else 0
    for which in (0, 1):
        for start in range(0, full, 256):
            pieces.append([(which, start, 256)])
    if width > full:
        if (width - full) % LANES == 0:
            pieces.append([(0, full, width - full), (1, full, width - full)])
        else:
            pieces.append([(0, full, width - full)])
            pieces.append([(1, full, width - full)])
    return pieces


def kernel(
    n, chunks, fold,
    req, tok, gate, up, amap, bmap, out,
    xall, xs, gv, uv, av, bg, bu, acc, accl, packed, lg, lu,
    tok_sem, w_sem, b_sem, ring_send, ring_recv, sib_send, sib_recv, low_send, low_recv,
):
    depth, width = gate.shape
    own_rows = tok.shape[0]
    rows = n * own_rows
    slots = MOST * SEQ
    chips = n // 2
    kc = depth // chunks
    rank = bmap.shape[2]
    per = LANES // rank
    me = lax.axis_index("tensor")
    core = me % 2
    chip = me // 2

    def chip_at(p):
        p = (p + chips) % chips
        if not fold:
            return p
        y = p // (chips // 2)
        return 2 * (p + y * (chips - 1 - 2 * p)) + y

    if fold:
        pos = chip // 2 + (chip % 2) * (chips - 1 - 2 * (chip // 2))
    else:
        pos = chip
    right = chip_at(pos + 1) * 2 + core
    left = chip_at(pos - 1) * 2 + core
    sib = me + 1 - 2 * core

    def columns(c):
        return pl.ds(0, LANES + kc) if c == 0 else pl.ds(LANES + c * kc, kc)

    def weights(c):
        span = pl.ds(c * kc, kc)
        return [
            pltpu.make_async_copy(amap.at[0, span], av.at[span], w_sem.at[c, 0]),
            pltpu.make_async_copy(gate.at[span], gv.at[span], w_sem.at[c, 1]),
            pltpu.make_async_copy(up.at[span], uv.at[span], w_sem.at[c, 2]),
        ]

    out_maps = [
        pltpu.make_async_copy(bmap.at[:, 0], bg, b_sem.at[0]),
        pltpu.make_async_copy(bmap.at[:, 1], bu, b_sem.at[1]),
    ]
    own_copy = pltpu.make_async_copy(tok, xall.at[me, :, pl.ds(LANES, depth)], tok_sem)
    own_copy.start()
    for copy in weights(0) + (weights(1) if chunks > 1 else []):
        copy.start()

    barrier = pltpu.get_barrier_semaphore()
    for off in range(1, n):
        pl.semaphore_signal(barrier, inc=1, device_id={"tensor": (me + off) % n}, device_id_type=MESH)

    row_of = lax.broadcasted_iota(jnp.int32, (own_rows, LANES), 0) // SEQ
    ids = jnp.zeros((own_rows, LANES), jnp.int32)
    for r in range(own_rows // SEQ):
        ids = jnp.where(row_of == r, req[r, 0], ids)
    xall[me, :, 0:LANES] = ids.astype(F32).astype(BF16)
    acc[...] = jnp.zeros_like(acc)
    accl[...] = jnp.zeros_like(accl)
    pl.semaphore_wait(barrier, n - 1)
    own_copy.wait()

    def block(owner, c):
        return xall.at[owner, :, columns(c)]

    def to_ring(way, c, s):
        owner = chip_at(pos - s if way == 0 else pos + s) * 2 + core
        return pltpu.make_async_remote_copy(
            src_ref=block(owner, c), dst_ref=block(owner, c),
            send_sem=ring_send.at[way, c, s], recv_sem=ring_recv.at[way, c, s],
            device_id={"tensor": right if way == 0 else left}, device_id_type=MESH,
        )

    def from_ring(way, c, s):
        owner = chip_at(pos - s - 1 if way == 0 else pos + s + 1) * 2 + core
        return pltpu.make_async_remote_copy(
            src_ref=block(owner, c), dst_ref=block(owner, c),
            send_sem=ring_send.at[way, c, s], recv_sem=ring_recv.at[way, c, s],
            device_id={"tensor": right if way == 0 else left}, device_id_type=MESH,
        )

    def to_sib(c, hop, whose):
        owner = chip_at(pos + hop) * 2 + whose
        return pltpu.make_async_remote_copy(
            src_ref=block(owner, c), dst_ref=block(owner, c),
            send_sem=sib_send.at[c, hop % chips], recv_sem=sib_recv.at[c, hop % chips],
            device_id={"tensor": sib}, device_id_type=MESH,
        )

    sent = []

    def go(copy):
        copy.start()
        sent.append(copy)

    def ring_step(c, s):
        ways = plan(chips, c)
        if s == 0:
            for way in (0, 1):
                if ways[way] > 0:
                    go(to_ring(way, c, 0))
            go(to_sib(c, 0, core))
            return
        for way in (0, 1):
            if s <= ways[way]:
                from_ring(way, c, s - 1).wait_recv()
                if s < ways[way]:
                    go(to_ring(way, c, s))
        for way in (0, 1):
            if s <= ways[way]:
                go(to_sib(c, -s if way == 0 else s, core))

    def gather_sib(c):
        ways = plan(chips, c)
        for hop in range(-ways[0], ways[1] + 1):
            to_sib(c, hop, 1 - core).wait_recv()

    def lay(c):
        base = LANES + c * kc
        xs[c % 2] = xall[:, :, base:base + kc].astype(F32).reshape(rows, kc).astype(BF16)

    pieces = pieces_of(width)

    def low_part(c):
        accl[...] += jnp.dot(xs[c % 2], av[c * kc:(c + 1) * kc], preferred_element_type=F32)

    def main_part(c):
        for i, piece in enumerate(pieces):
            cols = [
                (gv, uv)[which][c * kc:(c + 1) * kc, start:start + size]
                for which, start, size in piece
            ]
            w = cols[0] if len(cols) == 1 else jnp.concatenate(cols, axis=1)
            size = sum(part[2] for part in piece)
            acc[i, :, 0:size] += jnp.dot(xs[c % 2], w, preferred_element_type=F32)

    steps = max(plan(chips, 0))
    done = -1
    for tick in range(chunks + steps):
        for c in range(chunks):
            s = tick - c
            if 0 <= s <= steps:
                ring_step(c, s)
        ready = tick - steps - 1
        if ready >= 0:
            gather_sib(ready)
            lay(ready)
            for copy in weights(ready):
                copy.wait()
            low_part(ready)
            if ready < chunks - 2:
                main_part(ready)
        nxt = ready + 2
        if ready >= 0 and nxt < chunks:
            for copy in weights(nxt):
                copy.start()
        if nxt == chunks - 1:
            for copy in out_maps:
                copy.start()

    last = chunks - 1
    gather_sib(last)
    lay(last)
    for copy in weights(last):
        copy.wait()
    low_part(last)

    idw = xall[:, :, 0:LANES].astype(F32).reshape(rows, LANES)
    idc = idw[:, 0:1]
    idr = idw.T[0:1, :]
    same = idc == idr
    at_row = lax.broadcasted_iota(jnp.int32, (rows, rows), 0)
    at_col = lax.broadcasted_iota(jnp.int32, (rows, rows), 1)
    place_r = jnp.sum(jnp.where(same & (at_row < at_col), 1.0, 0.0), axis=0, keepdims=True)
    dest_r = (idr * slots + place_r).astype(jnp.int32)
    slot_of = lax.broadcasted_iota(jnp.int32, (slots, rows), 0) + me * slots
    pick = jnp.where(slot_of == dest_r, 1.0, 0.0).astype(BF16)
    low_own = accl[...].astype(BF16)
    packed[me] = jnp.dot(pick, low_own, preferred_element_type=F32).astype(BF16)

    def low_copy(off, owner):
        return pltpu.make_async_remote_copy(
            src_ref=packed.at[owner], dst_ref=packed.at[owner],
            send_sem=low_send.at[off], recv_sem=low_recv.at[off],
            device_id={"tensor": (me + off) % n}, device_id_type=MESH,
        )

    for off in range(1, n):
        go(low_copy(off, me))

    if chunks > 1:
        main_part(last - 1)
    main_part(last)
    place_c = jnp.sum(jnp.where(same & (at_col < at_row), 1.0, 0.0), axis=1, keepdims=True)
    dest_c = (idc * slots + place_c).astype(jnp.int32)
    spread = jnp.where(
        lax.broadcasted_iota(jnp.int32, (rows, n * slots), 1) == dest_c, 1.0, 0.0
    ).astype(BF16)
    for copy in out_maps:
        copy.wait()
    for off in range(1, n):
        low_copy(off, (me - off + n) % n).wait_recv()
    low = jnp.dot(spread, packed[...].reshape(n * slots, LANES), preferred_element_type=F32)
    idi = idc.astype(jnp.int32)
    group = lax.broadcasted_iota(jnp.int32, (rows, LANES), 1) // rank
    for which, dst in ((0, lg), (1, lu)):
        part = low[:, which * rank:(which + 1) * rank]
        twice = jnp.concatenate([part] * per, axis=1)
        for j in range(n // per):
            dst[:, j * LANES:(j + 1) * LANES] = jnp.where(
                group + j * per == idi, twice, 0.0
            ).astype(BF16)

    where_is = {}
    for i, piece in enumerate(pieces):
        offset = 0
        for which, start, size in piece:
            where_is[which, start] = (i, offset, size)
            offset += size
    for (which, start), (i, offset, size) in list(where_is.items()):
        if which:
            continue
        totals = []
        for kind, left_side, maps in ((0, lg, bg), (1, lu, bu)):
            j, off, _ = where_is[kind, start]
            totals.append(
                acc[j, :, off:off + size]
                + jnp.dot(
                    left_side[...],
                    maps[:, :, start:start + size].reshape(n * rank, size),
                    preferred_element_type=F32,
                )
            )
        g, u = totals
        out[:, start:start + size] = (g / (1.0 + jnp.exp(-g)) * u).astype(out.dtype)

    for copy in sent:
        copy.wait_send()


def local(tokens, gate_matrix, up_matrix, adapter_input_maps, adapter_output_maps, request_adapter):
    n = lax.axis_size("tensor")
    depth, width = gate_matrix.shape
    own_rows = tokens.shape[0]
    rows = n * own_rows
    rank = adapter_output_maps.shape[2]
    chips = n // 2
    chunks = 4
    kc = depth // chunks
    steps = chips // 2 + 1
    pieces = pieces_of(width)
    wide = max(sum(part[2] for part in piece) for piece in pieces)
    dma = pltpu.SemaphoreType.DMA
    anyspace = pl.BlockSpec(memory_space=pl.ANY)
    flops = 2 * rows * depth * (2 * width + 2 * rank)
    return pl.pallas_call(
        functools.partial(kernel, n, chunks, chips == 8),
        out_shape=jax.ShapeDtypeStruct((rows, width), BF16),
        in_specs=[pl.BlockSpec(memory_space=pltpu.SMEM)] + [anyspace] * 5,
        out_specs=pl.BlockSpec(memory_space=pltpu.VMEM),
        scratch_shapes=[
            pltpu.VMEM((n, own_rows, LANES + depth), BF16),
            pltpu.VMEM((2, rows, kc), BF16),
            pltpu.VMEM((depth, width), BF16),
            pltpu.VMEM((depth, width), BF16),
            pltpu.VMEM((depth, LANES), BF16),
            pltpu.VMEM((n, rank, width), BF16),
            pltpu.VMEM((n, rank, width), BF16),
            pltpu.VMEM((len(pieces), rows, wide), F32),
            pltpu.VMEM((rows, LANES), F32),
            pltpu.VMEM((n, MOST * SEQ, LANES), BF16),
            pltpu.VMEM((rows, n * rank), BF16),
            pltpu.VMEM((rows, n * rank), BF16),
            dma,
            dma((chunks, 3)),
            dma((2,)),
            dma((2, chunks, steps)),
            dma((2, chunks, steps)),
            dma((chunks, chips)),
            dma((chunks, chips)),
            dma((n,)),
            dma((n,)),
        ],
        compiler_params=pltpu.CompilerParams(
            collective_id=0, has_side_effects=True, vmem_limit_bytes=60 * 1024 * 1024
        ),
        cost_estimate=pl.CostEstimate(
            flops=flops, bytes_accessed=4 * depth * width, transcendentals=rows * width
        ),
    )(request_adapter, tokens, gate_matrix, up_matrix, adapter_input_maps, adapter_output_maps)


def solution(mesh):
    in_specs = (
        P(("groups", "tensor"), None),
        P(None, "tensor"),
        P(None, "tensor"),
        P("tensor", None, None),
        P(None, None, None, "tensor"),
        P(("groups", "tensor"), None),
    )
    out_specs = P("groups", "tensor")
    return jax.shard_map(local, mesh=mesh, in_specs=in_specs, out_specs=out_specs, check_vma=False)
```

```python
import functools

import jax
import jax.numpy as jnp
from jax import lax
from jax.experimental import pallas as pl
from jax.experimental.pallas import tpu as pltpu
from jax.sharding import PartitionSpec as P

SEQ = 4
MOST = 8
LANES = 128
MESH = pl.DeviceIdType.MESH
F32 = jnp.float32
BF16 = jnp.bfloat16


def pieces_of(width):
    pieces = []
    full = width // 256 * 256 if width >= 256 else 0
    for which in (0, 1):
        for start in range(0, full, 256):
            pieces.append([(which, start, 256)])
    if width > full:
        if (width - full) % LANES == 0:
            pieces.append([(0, full, width - full), (1, full, width - full)])
        else:
            pieces.append([(0, full, width - full)])
            pieces.append([(1, full, width - full)])
    return pieces


def kernel(
    n, chunks, ny,
    req, tok, gate, up, amap, bmap, out,
    xall, xs, gv, uv, av, bg, bu, acc, accl, packed, lg, lu,
    tok_sem, w_sem, b_sem, z_send, z_recv, y_send, y_recv, sib_send, sib_recv,
    low_send, low_recv, pair_send, pair_recv,
):
    depth, width = gate.shape
    own_rows = tok.shape[0]
    rows = n * own_rows
    slots = MOST * SEQ
    chips = n // 2
    kc = depth // chunks
    rank = bmap.shape[2]
    per = LANES // rank
    me = lax.axis_index("tensor")
    core = me % 2
    nz = n // (2 * ny)
    y, z = (me // 2) % ny, me // (2 * ny)

    def device(zz, yy, cc):
        return (zz * ny + yy) * 2 + cc

    order = [(d % 2, (d // 2) % ny, d // (2 * ny)) for d in range(n)]
    sib = me + 1 - 2 * core

    def columns(c):
        return pl.ds(0, LANES + kc) if c == 0 else pl.ds(LANES + c * kc, kc)

    def weights(c):
        span = pl.ds(c * kc, kc)
        return [
            pltpu.make_async_copy(amap.at[0, span], av.at[span], w_sem.at[c, 0]),
            pltpu.make_async_copy(gate.at[span], gv.at[span], w_sem.at[c, 1]),
            pltpu.make_async_copy(up.at[span], uv.at[span], w_sem.at[c, 2]),
        ]

    out_maps = [
        pltpu.make_async_copy(bmap.at[:, 0], bg, b_sem.at[0]),
        pltpu.make_async_copy(bmap.at[:, 1], bu, b_sem.at[1]),
    ]
    own_copy = pltpu.make_async_copy(tok, xall.at[core, y, z, :, pl.ds(LANES, depth)], tok_sem)
    own_copy.start()

    barrier = pltpu.get_barrier_semaphore()
    peers = [
        (dz, dy) for dz in range(nz) for dy in range(ny) if dz or dy
    ]

    def peer(dz, dy):
        return (z + dz) % nz, (y + dy) % ny

    for dz, dy in peers:
        pl.semaphore_signal(
            barrier, inc=1, device_id={"tensor": device(*peer(dz, dy), core)}, device_id_type=MESH
        )
    pl.semaphore_signal(barrier, inc=1, device_id={"tensor": sib}, device_id_type=MESH)

    row_of = lax.broadcasted_iota(jnp.int32, (own_rows, LANES), 0) // SEQ
    ids = jnp.zeros((own_rows, LANES), jnp.int32)
    for r in range(own_rows // SEQ):
        ids = jnp.where(row_of == r, req[0, r], ids)
    xall[core, y, z, :, 0:LANES] = ids.astype(F32).astype(BF16)
    acc[...] = jnp.zeros_like(acc)
    accl[...] = jnp.zeros_like(accl)
    pl.semaphore_wait(barrier, len(peers) + 1)
    own_copy.wait()

    def remote(ref, send, recv, target):
        return pltpu.make_async_remote_copy(
            src_ref=ref, dst_ref=ref, send_sem=send, recv_sem=recv,
            device_id={"tensor": target}, device_id_type=MESH,
        )

    sent = []

    def go(copy):
        copy.start()
        sent.append(copy)

    def z_copy(c, dz, zz):
        ref = xall.at[core, y, zz, :, columns(c)]
        return remote(ref, z_send.at[c, dz], z_recv.at[c, dz], device((z + dz) % nz, y, core))

    def y_copy(c, yy, dz):
        ref = xall.at[core, yy, (z - dz + nz) % nz, :, columns(c)]
        return remote(ref, y_send.at[c, dz], y_recv.at[c, dz], device(z, (y + 1) % ny, core))

    def sib_copy(c, cc, dy):
        ref = xall.at[cc, (y + dy) % ny, :, :, columns(c)]
        return remote(ref, sib_send.at[c, dy], sib_recv.at[c, dy], sib)

    def stage_z(c):
        for dz in range(1, nz):
            z_copy(c, dz, (z - dz + nz) % nz).wait_recv()
            if ny > 1:
                go(y_copy(c, y, dz))
        go(sib_copy(c, core, 0))

    def stage_y(c):
        if ny > 1:
            for dz in range(nz):
                y_copy(c, (y + 1) % ny, dz).wait_recv()
            go(sib_copy(c, core, 1))

    def gather_sib(c):
        for dy in range(ny):
            sib_copy(c, 1 - core, dy).wait_recv()

    def rows_of(cols):
        return jnp.concatenate([xall[k, i, j, :, cols].astype(F32) for k, i, j in order], axis=0)

    def lay(c):
        base = LANES + c * kc
        xs[c % 2] = rows_of(slice(base, base + kc)).astype(BF16)

    pieces = pieces_of(width)

    def low_part(c):
        accl[...] += jnp.dot(xs[c % 2], av[c * kc:(c + 1) * kc], preferred_element_type=F32)

    def main_part(c, first=0, stop=None):
        for i, piece in list(enumerate(pieces))[first:stop]:
            cols = [
                (gv, uv)[which][c * kc:(c + 1) * kc, start:start + size]
                for which, start, size in piece
            ]
            w = cols[0] if len(cols) == 1 else jnp.concatenate(cols, axis=1)
            size = sum(part[2] for part in piece)
            acc[i, :, 0:size] += jnp.dot(xs[c % 2], w, preferred_element_type=F32)

    for c in range(chunks):
        for dz in range(1, nz):
            go(z_copy(c, dz, z))
        if ny > 1:
            go(y_copy(c, y, 0))
    for copy in weights(0) + (weights(1) if chunks > 1 else []):
        copy.start()
    for tick in range(chunks + 1):
        if tick < chunks:
            stage_z(tick)
        if 1 <= tick:
            stage_y(tick - 1)
        ready = tick - 2
        if ready >= 0:
            gather_sib(ready)
            lay(ready)
            for copy in weights(ready):
                copy.wait()
            low_part(ready)
            main_part(ready)
        nxt = ready + 2
        if ready >= 0 and nxt < chunks:
            for copy in weights(nxt):
                copy.start()
        if nxt == max(chunks - 1, 1):
            for copy in out_maps:
                copy.start()

    last = chunks - 1
    idw = rows_of(slice(0, LANES))
    idc = idw[:, 0:1]
    idr = idw.T[0:1, :]
    same = idc == idr
    at_row = lax.broadcasted_iota(jnp.int32, (rows, rows), 0)
    at_col = lax.broadcasted_iota(jnp.int32, (rows, rows), 1)
    place_r = jnp.sum(jnp.where(same & (at_row < at_col), 1.0, 0.0), axis=0, keepdims=True)
    dest_r = (idr * slots + place_r).astype(jnp.int32)
    slot_of = lax.broadcasted_iota(jnp.int32, (slots, rows), 0) + me * slots
    pick = jnp.where(slot_of == dest_r, 1.0, 0.0).astype(BF16)
    place_c = jnp.sum(jnp.where(same & (at_col < at_row), 1.0, 0.0), axis=1, keepdims=True)
    dest_c = (idc * slots + place_c).astype(jnp.int32)
    spread = jnp.where(
        lax.broadcasted_iota(jnp.int32, (rows, n * slots), 1) == dest_c, 1.0, 0.0
    ).astype(BF16)
    idi = idc.astype(jnp.int32)
    group = lax.broadcasted_iota(jnp.int32, (rows, LANES), 1) // rank
    gather_sib(last)
    lay(last)
    for copy in weights(last):
        copy.wait()
    low_part(last)

    low_own = accl[...].astype(BF16)
    packed[core, y, z] = jnp.dot(pick, low_own, preferred_element_type=F32).astype(BF16)

    def low_copy(i, zz, yy):
        dz, dy = peers[i]
        ref = packed.at[core, yy, zz]
        return remote(ref, low_send.at[i], low_recv.at[i], device(*peer(dz, dy), core))

    for i in range(len(peers)):
        go(low_copy(i, z, y))
    early = len(pieces) // 2
    main_part(last, 0, early)
    for i, (dz, dy) in enumerate(peers):
        low_copy(i, (z - dz + nz) % nz, (y - dy + ny) % ny).wait_recv()

    def pair_copy(cc):
        return remote(packed.at[cc], pair_send, pair_recv, sib)

    go(pair_copy(core))
    main_part(last, early, len(pieces))
    for copy in out_maps:
        copy.wait()
    pair_copy(1 - core).wait_recv()
    table = jnp.concatenate([packed[k, i, j] for k, i, j in order], axis=0)
    low = jnp.dot(spread, table, preferred_element_type=F32)
    for which, dst in ((0, lg), (1, lu)):
        part = low[:, which * rank:(which + 1) * rank]
        twice = jnp.concatenate([part] * per, axis=1)
        for j in range(n // per):
            dst[:, j * LANES:(j + 1) * LANES] = jnp.where(
                group + j * per == idi, twice, 0.0
            ).astype(BF16)

    where_is = {}
    for i, piece in enumerate(pieces):
        offset = 0
        for which, start, size in piece:
            where_is[which, start] = (i, offset, size)
            offset += size
    for (which, start), (i, offset, size) in list(where_is.items()):
        if which:
            continue
        totals = []
        for kind, left_side, maps in ((0, lg, bg), (1, lu, bu)):
            j, off, _ = where_is[kind, start]
            totals.append(
                acc[j, :, off:off + size]
                + jnp.dot(
                    left_side[...],
                    maps[:, :, start:start + size].reshape(n * rank, size),
                    preferred_element_type=F32,
                )
            )
        g, u = totals
        out[:, start:start + size] = (g / (1.0 + jnp.exp(-g)) * u).astype(out.dtype)

    for copy in sent:
        copy.wait_send()


def local(tokens, gate_matrix, up_matrix, adapter_input_maps, adapter_output_maps, request_adapter):
    n = lax.axis_size("tensor")
    depth, width = gate_matrix.shape
    own_rows = tokens.shape[0]
    rows = n * own_rows
    rank = adapter_output_maps.shape[2]
    chips = n // 2
    chunks = 4
    kc = depth // chunks
    ny = 2 if chips == 8 else 1
    nz = chips // ny
    pieces = pieces_of(width)
    wide = max(sum(part[2] for part in piece) for piece in pieces)
    dma = pltpu.SemaphoreType.DMA
    anyspace = pl.BlockSpec(memory_space=pl.ANY)
    flops = 2 * rows * depth * (2 * width + 2 * rank)
    return pl.pallas_call(
        functools.partial(kernel, n, chunks, ny),
        out_shape=jax.ShapeDtypeStruct((rows, width), BF16),
        in_specs=[pl.BlockSpec(memory_space=pltpu.SMEM)] + [anyspace] * 5,
        out_specs=pl.BlockSpec(memory_space=pltpu.VMEM),
        scratch_shapes=[
            pltpu.VMEM((2, ny, nz, own_rows, LANES + depth), BF16),
            pltpu.VMEM((2, rows, kc), BF16),
            pltpu.VMEM((depth, width), BF16),
            pltpu.VMEM((depth, width), BF16),
            pltpu.VMEM((depth, LANES), BF16),
            pltpu.VMEM((n, rank, width), BF16),
            pltpu.VMEM((n, rank, width), BF16),
            pltpu.VMEM((len(pieces), rows, wide), F32),
            pltpu.VMEM((rows, LANES), F32),
            pltpu.VMEM((2, ny, nz, MOST * SEQ, LANES), BF16),
            pltpu.VMEM((rows, n * rank), BF16),
            pltpu.VMEM((rows, n * rank), BF16),
            dma,
            dma((chunks, 3)),
            dma((2,)),
            dma((chunks, nz)),
            dma((chunks, nz)),
            dma((chunks, nz)),
            dma((chunks, nz)),
            dma((chunks, ny)),
            dma((chunks, ny)),
            dma((chips,)),
            dma((chips,)),
            dma,
            dma,
        ],
        compiler_params=pltpu.CompilerParams(
            collective_id=0, has_side_effects=True, vmem_limit_bytes=60 * 1024 * 1024
        ),
        cost_estimate=pl.CostEstimate(
            flops=flops, bytes_accessed=4 * depth * width, transcendentals=rows * width
        ),
    )(request_adapter.T, tokens, gate_matrix, up_matrix, adapter_input_maps, adapter_output_maps)


def solution(mesh):
    in_specs = (
        P(("groups", "tensor"), None),
        P(None, "tensor"),
        P(None, "tensor"),
        P("tensor", None, None),
        P(None, None, None, "tensor"),
        P(("groups", "tensor"), None),
    )
    out_specs = P("groups", "tensor")
    return jax.shard_map(local, mesh=mesh, in_specs=in_specs, out_specs=out_specs, check_vma=False)
```
